32 devices in a mesh: fsdp: 8 (over z, y), rep: 4 (over x, core).
Axes of the slice: x: 2, y: 2, z: 4, core: 2. Of those that a mesh axis runs over, the one named last changes fastest.
Arguments:
- latents: bfloat16 [3, 64, 256, 384], P(None, ('fsdp', 'rep')), may hold values from -6 to 6
- cotangent: bfloat16 [3, 64, 256, 384], P(None, ('fsdp', 'rep')), may hold values from -6 to 6
- counts: int32 [3, 32], P(None, ('fsdp', 'rep')), may hold values from 1 to 2, 48 in all within a row
- labels: int32 [3, 64], P(None, ('fsdp', 'rep')), may hold values from 0 to 999
- timesteps: int32 [3, 64], P(None, ('fsdp', 'rep')), may hold values from 0 to 999
- class_table: bfloat16 [1000, 384], P(None, 'fsdp'), may hold values from -5 to 5
- time_table: bfloat16 [1000, 384], P(None, 'fsdp'), may hold values from -5 to 5
- ada_weight: bfloat16 [2, 384, 2304], P(None, 'fsdp'), may hold values from -0.3125 to 0.3125
- ada_bias: bfloat16 [2, 2304], P(None, 'fsdp'), may hold values from -3 to 3
- qkv_weight: bfloat16 [2, 384, 1152], P(None, 'fsdp'), may hold values from -0.3125 to 0.3125
- qv_bias: bfloat16 [2, 768], P(None, 'fsdp'), may hold values from -3 to 3
- proj_weight: bfloat16 [2, 384, 384], P(None, 'fsdp'), may hold values from -1.25 to 1.25
- proj_bias: bfloat16 [2, 384], P(None, 'fsdp'), may hold values from -3 to 3
- fc1_weight: bfloat16 [2, 384, 1536], P(None, 'fsdp'), may hold values from -0.3125 to 0.3125
- fc1_bias: bfloat16 [2, 1536], P(None, 'fsdp'), may hold values from -3 to 3
- fc2_weight: bfloat16 [2, 1536, 384], P(None, 'fsdp'), may hold values from -0.15625 to 0.15625
- fc2_bias: bfloat16 [2, 384], P(None, 'fsdp'), may hold values from -3 to 3
Outputs:
- outputs: bfloat16 [3, 64, 256, 384], P(None, ('fsdp', 'rep'))
- input_grad: bfloat16 [3, 64, 256, 384], P(None, ('fsdp', 'rep'))
- class_grad: float32 [1000, 384], P(None, 'fsdp')
- time_grad: float32 [1000, 384], P(None, 'fsdp')
- ada_weight_grad: float32 [2, 384, 2304], P(None, 'fsdp')
- ada_bias_grad: float32 [2, 2304], P(None, 'fsdp')
- qkv_weight_grad: float32 [2, 384, 1152], P(None, 'fsdp')
- qv_bias_grad: float32 [2, 768], P(None, 'fsdp')
- proj_weight_grad: float32 [2, 384, 384], P(None, 'fsdp')
- proj_bias_grad: float32 [2, 384], P(None, 'fsdp')
- fc1_weight_grad: float32 [2, 384, 1536], P(None, 'fsdp')
- fc1_bias_grad: float32 [2, 1536], P(None, 'fsdp')
- fc2_weight_grad: float32 [2, 1536, 384], P(None, 'fsdp')
- fc2_bias_grad: float32 [2, 384], P(None, 'fsdp')
The draws below stay inside these ranges and needn't reach their ends.
Inputs may be any that keep to these rules, and one draw needn't show every extreme that they name: A device's live latents are its first slots; the counts of one micro-batch add up to 48, and some device holds 2.
All inputs are finite; a program needn't handle non-finite values.
Results may differ from the reference program's by a relative error of at most 0.017.
Values may be sent and summed in bfloat16 or wider, within the bound.
A program may use at most 192 MiB of HBM per device.

```python
import math
import jax
import jax.numpy as jnp
import numpy as np
from jax import lax

D = 384
HEADS = 6
FF = 1536
CLASSES = 1000
STEPS = 1000
TOK = 256
LAYERS = 2
MICRO = 3
SLOTS = 2
LATENTS = 64
DEVICES = 32


def with_ends(entries, own_key, low, high):
    longest = entries.shape.index(max(entries.shape))
    spots = []
    for shift in (0, 1):
        where = [jax.random.randint(jax.random.fold_in(own_key, axis), (), 0, length) for axis, length in enumerate(entries.shape)]
        where[longest] = (where[longest] + shift) % entries.shape[longest]
        spots.append(tuple(where))
    return entries.at[spots[0]].set(low).at[spots[1]].set(high)


def block_levels(key, extent, cuts, low, high):
    gain, own = 1.0, jax.random.fold_in(key, 6)
    for axis_at, shards_of in cuts:
        draws = jnp.exp(jax.random.uniform(jax.random.fold_in(own, axis_at), (shards_of,), jnp.float32, low / len(cuts), high / len(cuts)))
        gain = gain * jnp.repeat(draws, extent[axis_at] // shards_of).reshape([-1 if axis == axis_at else 1 for axis in range(len(extent))])
    return gain


def length_profile(amount, total, reach, skew):
    loads = [(1 << 20) // math.isqrt(rank ** skew) + 1 for rank in range(2, amount + 1)]
    spare, holding = total - reach - (amount - 1), [1] * (amount - 1)
    while spare > 0:
        free = [i for i in range(amount - 1) if holding[i] < reach]
        mass, budget = sum([loads[i] for i in free]), spare
        for i in free:
            addition = min(reach - holding[i], max(1, budget * loads[i] // mass), spare)
            holding[i] = holding[i] + addition
            spare = spare - addition
    return np.array([reach] + holding)


def ragged(own_key, count, total, limit, lean):
    if count == 2:
        one = jax.random.randint(own_key, (), max(1, total - limit), min(limit, total - 1) + 1)
        return jnp.stack([one, total - one])
    tallies = jnp.asarray(length_profile(count, total, limit, lean), jnp.int32)
    twos = (count - 1) // 2
    giver, receiver = tallies[1:1 + 2 * twos:2], tallies[2:2 + 2 * twos:2]
    margin = jnp.minimum(giver - 1, limit - receiver)
    moved = jax.random.randint(jax.random.fold_in(own_key, 1), (twos,), 0, 1 << 20) % (margin + 1)
    tallies = tallies.at[1:1 + 2 * twos:2].set(giver - moved).at[2:2 + 2 * twos:2].set(receiver + moved)
    return tallies[jax.random.permutation(jax.random.fold_in(own_key, 2), count)]


def noise(key, shape, scale, most, shards=(), held_as=jnp.bfloat16):
    array = scale * jax.random.normal(key, shape, jnp.float32)
    if shards:
        array = array * block_levels(key, shape, shards, -0.22, 0.18)
    return jnp.clip(array, -most, most).astype(held_as)


def setup_inputs(seed: int = 0) -> dict:
    arg_keys = jax.random.split(jax.random.key(seed), 18)
    latents = noise(arg_keys[0], (MICRO, LATENTS, TOK, D), 1.0, 6.0, ((1, 32),))
    cotangent = noise(arg_keys[1], (MICRO, LATENTS, TOK, D), 1.0, 6.0, ((1, 32),))
    counts = jax.vmap(lambda own: ragged(own, DEVICES, (SLOTS + 1) * DEVICES // 2, SLOTS, 2))(jax.random.split(arg_keys[2], MICRO)).reshape((MICRO, DEVICES)).astype(jnp.int32)
    labels = with_ends(jax.random.randint(arg_keys[3], (MICRO, LATENTS), 0, CLASSES), jax.random.fold_in(arg_keys[3], 1), 0, CLASSES - 1).astype(jnp.int32)
    timesteps = with_ends(jax.random.randint(arg_keys[4], (MICRO, LATENTS), 0, STEPS), jax.random.fold_in(arg_keys[4], 1), 0, STEPS - 1).astype(jnp.int32)
    class_table = noise(arg_keys[5], (CLASSES, D), 0.8, 5.0, ((1, 8),))
    time_table = noise(arg_keys[6], (STEPS, D), 0.8, 5.0, ((1, 8),))
    ada_weight = noise(arg_keys[7], (LAYERS, D, 6 * D), D ** -0.5, 0.3125, ((1, 8),))
    ada_bias = noise(arg_keys[8], (LAYERS, 6 * D), 0.5, 3.0, ((1, 8),))
    qkv_weight = noise(arg_keys[9], (LAYERS, D, 3 * D), D ** -0.5, 0.3125, ((1, 8),))
    qv_bias = noise(arg_keys[10], (LAYERS, 2 * D), 0.5, 3.0, ((1, 8),))
    proj_weight = noise(arg_keys[11], (LAYERS, D, D), (D // 16) ** -0.5, 1.25, ((1, 8),))
    proj_bias = noise(arg_keys[12], (LAYERS, D), 0.4, 3.0, ((1, 8),))
    fc1_weight = noise(arg_keys[13], (LAYERS, D, FF), D ** -0.5, 0.3125, ((1, 8),))
    fc1_bias = noise(arg_keys[14], (LAYERS, FF), 0.5, 3.0, ((1, 8),))
    fc2_weight = noise(arg_keys[15], (LAYERS, FF, D), FF ** -0.5, 0.15625, ((1, 8),))
    fc2_bias = noise(arg_keys[16], (LAYERS, D), 0.4, 3.0, ((1, 8),))
    return dict(latents=latents, cotangent=cotangent, counts=counts, labels=labels, timesteps=timesteps, class_table=class_table, time_table=time_table, ada_weight=ada_weight, ada_bias=ada_bias, qkv_weight=qkv_weight, qv_bias=qv_bias, proj_weight=proj_weight, proj_bias=proj_bias, fc1_weight=fc1_weight, fc1_bias=fc1_bias, fc2_weight=fc2_weight, fc2_bias=fc2_bias)


@jax.custom_vjp
def low(v):
    return lax.optimization_barrier(v.astype(jnp.bfloat16)).astype(jnp.float32)

@jax.custom_vjp
def low_back(v):
    return v

def low_keep(v):
    return (low(v), None)

def low_pass(kept, grad):
    return (grad,)

def back_keep(v):
    return (v, None)

def back_low(kept, grad):
    return (low(grad),)
low.defvjp(low_keep, low_pass)
low_back.defvjp(back_keep, back_low)
highest = lax.Precision.HIGHEST
epsilon = 1e-06

def layer_norm(values):
    centre = lax.optimization_barrier(jnp.mean(values, axis=-1, keepdims=True))
    centred = values - centre
    spread = lax.optimization_barrier(jnp.mean(centred * centred, axis=-1, keepdims=True))
    return centred * lax.rsqrt(spread + epsilon)

def project(moved, matrix):
    return jnp.einsum('std,de->ste', moved, matrix, precision=highest)

def transformer_layer_list(model_parameters, block_input_state, condition_vector):
    ada_w, ada_b, qkv_w, qv_b, proj_w, proj_b, fc1_w, fc1_b, fc2_w, fc2_b = model_parameters
    latent_count, length, features = block_input_state.shape
    head_size = features // HEADS
    score_scale = head_size ** (-0.5)
    lifted = low(jax.nn.silu(condition_vector))
    residual = block_input_state
    for layer_index in range(LAYERS):
        modulation = jnp.dot(lifted, ada_w[layer_index], precision=highest) + ada_b[layer_index]
        pieces = [modulation[:, None, column * features:(column + 1) * features] for column in range(6)]
        shift_a, scale_a, gate_a, shift_m, scale_m, gate_m = pieces
        moved_a = low(layer_norm(residual) * (1.0 + scale_a) + shift_a)
        projected = project(moved_a, qkv_w[layer_index])
        queries = low(low_back(projected[..., :features] + qv_b[layer_index, :features]))
        key_rows = low(low_back(projected[..., features:2 * features]))
        value_rows = low(low_back(projected[..., 2 * features:] + qv_b[layer_index, features:]))
        queries = queries.reshape(latent_count, length, HEADS, head_size)
        key_rows = key_rows.reshape(latent_count, length, HEADS, head_size)
        value_rows = value_rows.reshape(latent_count, length, HEADS, head_size)
        scores = low_back(jnp.einsum('sqhe,skhe->shqk', queries, key_rows, precision=highest) * score_scale)
        soft_r = low(jax.nn.softmax(scores, axis=-1))
        blended = jnp.einsum('shqk,skhe->sqhe', soft_r, value_rows, precision=highest)
        blended = low(low_back(blended.reshape(latent_count, length, features)))
        branch = low_back(project(blended, proj_w[layer_index]) + proj_b[layer_index])
        middle = residual + gate_a * branch
        moved_m = low(layer_norm(middle) * (1.0 + scale_m) + shift_m)
        hidden_input_rows = low_back(project(moved_m, fc1_w[layer_index]) + fc1_b[layer_index])
        hidden = low(jax.nn.gelu(hidden_input_rows, approximate=True))
        mlp_out = low_back(project(hidden, fc2_w[layer_index]) + fc2_b[layer_index])
        residual = middle + gate_m * mlp_out
    return residual

def reference(latents, cotangent, counts, labels, timesteps, class_table, time_table, ada_weight, ada_bias, qkv_weight, qv_bias, proj_weight, proj_bias, fc1_weight, fc1_bias, fc2_weight, fc2_bias):
    model_parameters = tuple((member.astype(jnp.float32) for member in (ada_weight, ada_bias, qkv_weight, qv_bias, proj_weight, proj_bias, fc1_weight, fc1_bias, fc2_weight, fc2_bias)))
    tables = (class_table.astype(jnp.float32), time_table.astype(jnp.float32))
    groups = MICRO * DEVICES
    inputs = latents.astype(jnp.float32).reshape(groups, SLOTS, TOK, D)
    incoming = cotangent.astype(jnp.float32).reshape(groups, SLOTS, TOK, D)
    slot_ids = jnp.arange(SLOTS, dtype=jnp.int32)
    living = (slot_ids[None, None, :] < counts[:, :, None]).astype(jnp.float32).reshape(groups, SLOTS)
    label_rows = labels.reshape(groups, SLOTS)
    step_rows = timesteps.reshape(groups, SLOTS)

    def one_group(totals, element):
        block_input_state, block_cot, active_latent_mask, label_ids, step_ids = element

        def forward(model_parameters, tables, block_input_state):
            condition_vector = tables[0][label_ids] + tables[1][step_ids]
            return transformer_layer_list(model_parameters, block_input_state, condition_vector) * active_latent_mask[:, None, None]
        result, pullback = jax.vjp(forward, model_parameters, tables, block_input_state)
        grad_params, grad_tables, grad_in = pullback(block_cot)
        totals = jax.tree.map(jnp.add, totals, (grad_params, grad_tables))
        return (totals, (result.astype(jnp.bfloat16), grad_in.astype(jnp.bfloat16)))
    initial = jax.tree.map(jnp.zeros_like, (model_parameters, tables))
    (grad_params, grad_tables), (outputs, grad_inputs) = lax.scan(one_group, initial, (inputs, incoming, living, label_rows, step_rows))
    out_shape = (MICRO, SLOTS * DEVICES, TOK, D)
    return (outputs.reshape(out_shape), grad_inputs.reshape(out_shape), grad_tables[0], grad_tables[1], grad_params[0], grad_params[1], grad_params[2], grad_params[3], grad_params[4], grad_params[5], grad_params[6], grad_params[7], grad_params[8], grad_params[9])
```

```python
from functools import partial

import jax
import jax.numpy as jnp
from jax import lax
from jax.experimental import pallas as pl
from jax.experimental.pallas import tpu as pltpu
from jax.sharding import PartitionSpec as P

HEADS = 6
LAYERS = 2
EPS = 1e-06
GELU_C = 0.7978845608028654
GELU_A = 0.044715
F32 = jnp.float32
BF16 = jnp.bfloat16


def dot(a, b, dims=((1,), (0,))):
    return lax.dot_general(a, b, (dims, ((), ())), preferred_element_type=F32)


def dot_nt(a, b):
    return dot(a, b, ((1,), (1,)))


def dot_tn(a, b):
    return dot(a, b, ((0,), (0,)))


def norm(x):
    centred = x - jnp.mean(x, axis=-1, keepdims=True)
    inv = lax.rsqrt(jnp.mean(centred * centred, axis=-1, keepdims=True) + EPS)
    return centred * inv, inv


def norm_back(n, inv, dn):
    return inv * (
        dn - jnp.mean(dn, axis=-1, keepdims=True) - n * jnp.mean(dn * n, axis=-1, keepdims=True)
    )


def col_sum(x):
    return jnp.sum(x, axis=0, keepdims=True)


def fwd_kernel(last, d, ff, live_ref, r_ref, mod_ref, wa_ref, wf2_ref, bias_ref,
               out_ref, qkv_ref, blend_ref, branch_ref, mid_ref, hin_ref, mlp_ref):
    mod = mod_ref[0]
    sh_a, sc_a, g_a, sh_m, sc_m, g_m = [mod[i : i + 1] for i in range(6)]
    hd = d // HEADS
    r = r_ref[0].astype(F32)
    n_a, _ = norm(r)
    moved = (n_a * (1.0 + sc_a) + sh_a).astype(BF16)
    q = dot(moved, wa_ref[:, :d]) + bias_ref[:, :d]
    k = dot(moved, wa_ref[:, d : 2 * d])
    v = dot(moved, wa_ref[:, 2 * d : 3 * d]) + bias_ref[:, d : 2 * d]
    q = q.astype(BF16)
    k = k.astype(BF16)
    v = v.astype(BF16)
    qkv_ref[0, :, :d] = q
    qkv_ref[0, :, d : 2 * d] = k
    qkv_ref[0, :, 2 * d :] = v
    qs = q * jnp.asarray(hd**-0.5, BF16)
    parts = []
    for h in range(HEADS):
        c = slice(h * hd, (h + 1) * hd)
        s = dot_nt(qs[:, c], k[:, c])
        e = jnp.exp(s - jnp.max(s, axis=-1, keepdims=True))
        inv = 1.0 / jnp.sum(e, axis=-1, keepdims=True)
        parts.append((dot(e.astype(BF16), v[:, c]) * inv).astype(BF16))
    blend = jnp.concatenate(parts, axis=1)
    blend_ref[0] = blend
    branch = dot(blend, wa_ref[:, 3 * d : 4 * d]) + bias_ref[:, 2 * d : 3 * d]
    branch_ref[0] = branch.astype(BF16)
    mid = r + g_a * branch
    mid_ref[0] = mid
    n_m, _ = norm(mid)
    moved = (n_m * (1.0 + sc_m) + sh_m).astype(BF16)
    hin = dot(moved, wa_ref[:, 4 * d :]) + bias_ref[:, 3 * d : 3 * d + ff]
    hin_ref[0] = hin.astype(BF16)
    t = jnp.tanh(GELU_C * (hin + GELU_A * hin * hin * hin))
    hidden = (0.5 * hin * (1.0 + t)).astype(BF16)
    mlp = dot(hidden, wf2_ref[...]) + bias_ref[:, 3 * d + ff :]
    mlp_ref[0] = mlp.astype(BF16)
    out = mid + g_m * mlp
    if last:
        out = jnp.where(live_ref[pl.program_id(0)] > 0, out, 0.0)
    out_ref[0] = out.astype(out_ref.dtype)


def bwd_kernel(first, last, d, ff, live_ref, g_ref, r_ref, mod_ref, wa_ref, wf2_ref,
               qkv_ref, blend_ref, branch_ref, mid_ref, hin_ref, mlp_ref,
               dr_ref, dmod_ref, dwa_ref, dwf2_ref, dbias_ref, acc_a, acc_f2):
    step = pl.program_id(0)

    @pl.when(step == 0)
    def _():
        acc_a[...] = jnp.zeros_like(acc_a)
        acc_f2[...] = jnp.zeros_like(acc_f2)
        dbias_ref[...] = jnp.zeros_like(dbias_ref)

    mod = mod_ref[0]
    _, sc_a, g_a, _, sc_m, g_m = [mod[i : i + 1] for i in range(6)]
    hd = d // HEADS
    g = g_ref[0].astype(F32)
    if last:
        g = jnp.where(live_ref[step] > 0, g, 0.0)
    dgm = col_sum(g * mlp_ref[0].astype(F32))
    gmlp_f = g_m * g
    dbias_ref[:, 3 * d + ff :] += col_sum(gmlp_f)
    gmlp = gmlp_f.astype(BF16)
    hin = hin_ref[0].astype(F32)
    sq = hin * hin
    t = jnp.tanh(GELU_C * hin * (1.0 + GELU_A * sq))
    half = 0.5 * (1.0 + t)
    hidden = (hin * half).astype(BF16)
    acc_f2[...] += dot_tn(hidden, gmlp)
    slope = half + (0.5 * GELU_C) * hin * (1.0 - t * t) * (1.0 + (3.0 * GELU_A) * sq)
    ghin_f = dot_nt(gmlp, wf2_ref[...]) * slope
    dbias_ref[:, 3 * d : 3 * d + ff] += col_sum(ghin_f)
    ghin = ghin_f.astype(BF16)
    n_m, inv_m = norm(mid_ref[0])
    mod_m = mod[3:4]
    moved = (n_m * (1.0 + sc_m) + mod_m).astype(BF16)
    acc_a[:, 4 * d :] += dot_tn(moved, ghin)
    gmoved = dot_nt(ghin, wa_ref[:, 4 * d :])
    dshm = col_sum(gmoved)
    dscm = col_sum(gmoved * n_m)
    gmid = g + norm_back(n_m, inv_m, gmoved * (1.0 + sc_m))
    dga = col_sum(gmid * branch_ref[0].astype(F32))
    gbr_f = g_a * gmid
    dbias_ref[:, 2 * d : 3 * d] += col_sum(gbr_f)
    gbr = gbr_f.astype(BF16)
    blend = blend_ref[0]
    acc_a[:, 3 * d : 4 * d] += dot_tn(blend, gbr)
    gbl = dot_nt(gbr, wa_ref[:, 3 * d : 4 * d]).astype(BF16)
    prod = gbl.astype(F32) * blend.astype(F32)
    q = qkv_ref[0, :, :d] * jnp.asarray(hd**-0.5, BF16)
    k = qkv_ref[0, :, d : 2 * d]
    v = qkv_ref[0, :, 2 * d :]
    dq, dk, dv = [], [], []
    for h in range(HEADS):
        c = slice(h * hd, (h + 1) * hd)
        s = dot_nt(q[:, c], k[:, c])
        e = jnp.exp(s - jnp.max(s, axis=-1, keepdims=True))
        soft = e * (1.0 / jnp.sum(e, axis=-1, keepdims=True))
        gs = dot_nt(gbl[:, c], v[:, c])
        dv.append(dot_tn(soft.astype(BF16), gbl[:, c]))
        ds = (soft * (gs - jnp.sum(prod[:, c], axis=-1, keepdims=True))).astype(BF16)
        dq.append(dot(ds, k[:, c]) * (hd**-0.5))
        dk.append(dot_tn(ds, q[:, c]))
    dq = jnp.concatenate(dq, axis=1)
    dk = jnp.concatenate(dk, axis=1)
    dv = jnp.concatenate(dv, axis=1)
    dbias_ref[:, :d] += col_sum(dq)
    dbias_ref[:, d : 2 * d] += col_sum(dv)
    dqkv = jnp.concatenate([dq, dk, dv], axis=1).astype(BF16)
    n_a, inv_a = norm(r_ref[0].astype(F32))
    moved = (n_a * (1.0 + sc_a) + mod[0:1]).astype(BF16)
    acc_a[:, : 3 * d] += dot_tn(moved, dqkv)
    gmoved = dot_nt(dqkv, wa_ref[:, : 3 * d])
    dsha = col_sum(gmoved)
    dsca = col_sum(gmoved * n_a)
    dr = gmid + norm_back(n_a, inv_a, gmoved * (1.0 + sc_a))
    dr_ref[0] = dr.astype(dr_ref.dtype)
    dmod_ref[0] = jnp.concatenate([dsha, dsca, dga, dshm, dscm, dgm], axis=0)

    @pl.when(step == pl.num_programs(0) - 1)
    def _():
        dwa_ref[...] = acc_a[...].astype(BF16)
        dwf2_ref[...] = acc_f2[...].astype(BF16)


def row_spec(*shape):
    return pl.BlockSpec((1,) + shape, lambda i: (i, 0, 0))


def full_spec(*shape):
    return pl.BlockSpec(shape, lambda i: (0,) * len(shape))


SMEM = pl.BlockSpec(memory_space=pltpu.SMEM)
PARAMS = pltpu.CompilerParams(
    dimension_semantics=("arbitrary",), vmem_limit_bytes=56 * 1024 * 1024
)


def layer_forward(last, live, r, mod, wa, wf2, bias):
    n, length, d = r.shape
    ff = wf2.shape[0]
    sds = jax.ShapeDtypeStruct
    return pl.pallas_call(
        partial(fwd_kernel, last, d, ff),
        grid=(n,),
        in_specs=[SMEM, row_spec(length, d), row_spec(6, d), full_spec(*wa.shape),
                  full_spec(*wf2.shape), full_spec(*bias.shape)],
        out_specs=[row_spec(length, d), row_spec(length, 3 * d), row_spec(length, d),
                   row_spec(length, d), row_spec(length, d), row_spec(length, ff),
                   row_spec(length, d)],
        out_shape=[
            sds((n, length, d), BF16 if last else F32),
            sds((n, length, 3 * d), BF16),
            sds((n, length, d), BF16),
            sds((n, length, d), BF16),
            sds((n, length, d), F32),
            sds((n, length, ff), BF16),
            sds((n, length, d), BF16),
        ],
        compiler_params=PARAMS,
        name="layer_forward",
    )(live, r, mod, wa, wf2, bias)


def layer_backward(first, last, live, g, r, mod, wa, wf2, saved):
    n, length, d = r.shape
    ff = wf2.shape[0]
    sds = jax.ShapeDtypeStruct
    width = 4 * d + ff
    return pl.pallas_call(
        partial(bwd_kernel, first, last, d, ff),
        grid=(n,),
        in_specs=[SMEM, row_spec(length, d), row_spec(length, d), row_spec(6, d),
                  full_spec(*wa.shape), full_spec(*wf2.shape), row_spec(length, 3 * d),
                  row_spec(length, d), row_spec(length, d), row_spec(length, d),
                  row_spec(length, ff), row_spec(length, d)],
        out_specs=[row_spec(length, d), row_spec(6, d), full_spec(d, width), full_spec(ff, d),
                   full_spec(1, 4 * d + ff)],
        out_shape=[
            sds((n, length, d), BF16 if first else F32),
            sds((n, 6, d), F32),
            sds((d, width), BF16),
            sds((ff, d), BF16),
            sds((1, 4 * d + ff), F32),
        ],
        scratch_shapes=[pltpu.VMEM((d, width), F32), pltpu.VMEM((ff, d), F32)],
        compiler_params=PARAMS,
        name="layer_backward",
    )(live, g, r, mod, wa, wf2, *saved)


def on_device(latents, cotangent, counts, labels, timesteps, class_table, time_table,
              ada_weight, ada_bias, qkv_weight, qv_bias, proj_weight, proj_bias,
              fc1_weight, fc1_bias, fc2_weight, fc2_bias):
    micro, slots, length, d = latents.shape
    n = micro * slots
    ff = fc1_weight.shape[2]
    owners = lax.axis_size("fsdp")
    me = lax.axis_index("fsdp")

    biases = (ada_bias, qv_bias, proj_bias, fc1_bias, fc2_bias)
    head = jnp.concatenate(
        [x.astype(F32).reshape(-1) for x in (labels, timesteps) + biases]
    )
    head = lax.all_gather(head, "fsdp")
    wa = []
    wf2 = []
    for l in range(LAYERS):
        packed = jnp.concatenate([qkv_weight[l], proj_weight[l], fc1_weight[l]], axis=1)
        wa.append(lax.all_gather(packed, "fsdp", axis=0, tiled=True))
        wf2.append(lax.all_gather(fc2_weight[l], "fsdp", axis=0, tiled=True))

    full_bias = []
    at = 2 * n
    for b in biases:
        w = b.shape[1]
        got = head[:, at : at + LAYERS * w].reshape(owners, LAYERS, w)
        full_bias.append(jnp.moveaxis(got, 0, 1).reshape(LAYERS, owners * w))
        at += LAYERS * w
    ada_b = full_bias[0]
    layer_bias = jnp.concatenate(full_bias[1:], axis=1)

    classes = class_table.shape[0]
    steps = time_table.shape[0]
    all_labels = head[:, :n].reshape(-1).astype(jnp.int32)
    all_steps = head[:, n : 2 * n].reshape(-1).astype(jnp.int32)
    label_hot = all_labels[:, None] == jnp.arange(classes, dtype=jnp.int32)[None, :]
    step_hot = all_steps[:, None] == jnp.arange(steps, dtype=jnp.int32)[None, :]
    cond = dot(label_hot.astype(BF16), class_table) + dot(step_hot.astype(BF16), time_table)
    sig = jax.nn.sigmoid(cond)
    lifted = (cond * sig).astype(BF16)
    part = jnp.concatenate([dot(lifted, ada_weight[l]) for l in range(LAYERS)], axis=1)
    mod = lax.psum_scatter(part, "fsdp", scatter_dimension=0, tiled=True)
    mod = mod.reshape(n, LAYERS, 6 * d) + ada_b[None]
    mod = [mod[:, l].reshape(n, 6, d) for l in range(LAYERS)]

    slot_ids = jnp.arange(slots, dtype=jnp.int32)
    live = (slot_ids[None, :] < counts).astype(jnp.int32).reshape(-1)

    r = latents.reshape(n, length, d)
    ins, saved = [], []
    for l in range(LAYERS):
        ins.append(r)
        r, *rest = layer_forward(
            l == LAYERS - 1, live, r, mod[l], wa[l], wf2[l], layer_bias[l][None]
        )
        saved.append(rest)
    outputs = r.reshape(latents.shape)

    g = cotangent.reshape(n, length, d)
    grads = [None] * LAYERS
    sums = [None] * LAYERS
    tails = [None] * LAYERS
    lift_grad = jnp.zeros(cond.shape, F32)
    for l in reversed(range(LAYERS)):
        g, dmod, dwa, dwf2, dbias = layer_backward(
            l == 0, l == LAYERS - 1, live, g, ins[l], mod[l], wa[l], wf2[l], saved[l]
        )
        dwa = lax.psum_scatter(dwa, "rep", scatter_dimension=1, tiled=True)
        dwa = lax.psum_scatter(dwa, "fsdp", scatter_dimension=0, tiled=True)
        dwf2 = dwf2.reshape(owners, ff // owners, d)
        dwf2 = lax.psum_scatter(dwf2, "rep", scatter_dimension=1, tiled=True)
        dwf2 = lax.psum_scatter(dwf2, "fsdp", scatter_dimension=0, tiled=True)[0]
        sums[l] = (dwa, dwf2)
        tails[l] = jnp.concatenate([dmod.reshape(-1), dbias.reshape(-1)]).astype(BF16)
    all_tails = lax.all_gather(jnp.stack(tails), "fsdp")
    for l in range(LAYERS):
        tail = all_tails[:, l]
        gmod = tail[:, : n * 6 * d].reshape(owners * n, 6 * d)
        gbias = jnp.sum(tail[:, n * 6 * d :].astype(F32), axis=0)
        dada = dot_tn(lifted, gmod)
        lift_grad = lift_grad + dot_nt(gmod, ada_weight[l])
        small = []
        at = 0
        for size in (2 * d, d, ff, d):
            own = size // owners
            small.append(lax.dynamic_slice(gbias, (at + me * own,), (own,)))
            at += size
        dada_b = jnp.sum(gmod.astype(F32), axis=0)
        own = 6 * d // owners
        small.append(lax.dynamic_slice(dada_b, (me * own,), (own,)))
        small = jnp.concatenate(small)
        grads[l] = (dada.astype(BF16), small.astype(BF16))
    full_a = lax.all_gather(jnp.stack([t[0] for t in sums]), "rep", axis=2, tiled=True)
    full_f2 = lax.all_gather(jnp.stack([t[1] for t in sums]), "rep", axis=1, tiled=True)
    full_a = full_a.astype(F32)
    input_grad = g.reshape(latents.shape)

    gcond = lift_grad * (sig * (1.0 + cond * (1.0 - sig)))
    hi = gcond.astype(BF16)
    lo = (gcond - hi.astype(F32)).astype(BF16)
    both = jnp.concatenate([hi, lo], axis=1)
    w = cond.shape[1]

    def scatter_rows(hot):
        out = dot_tn(hot.astype(BF16), both)
        return (out[:, :w] + out[:, w:]).astype(BF16)

    tables = (scatter_rows(label_hot), scatter_rows(step_hot))
    grads, tables = lax.psum((grads, tables), "rep")

    def stack(f):
        return jnp.stack([f(grads[l]).astype(F32) for l in range(LAYERS)])

    sizes = [2 * d // owners, d // owners, ff // owners, d // owners, 6 * d // owners]
    offs = [sum(sizes[:i]) for i in range(6)]
    sm = [stack(lambda t, i=i: t[1][offs[i] : offs[i + 1]]) for i in range(5)]
    return (
        outputs,
        input_grad,
        tables[0].astype(F32),
        tables[1].astype(F32),
        stack(lambda t: t[0]),
        sm[4],
        full_a[:, :, : 3 * d],
        sm[0],
        full_a[:, :, 3 * d : 4 * d],
        sm[1],
        full_a[:, :, 4 * d :],
        sm[2],
        full_f2.astype(F32),
        sm[3],
    )


def solution(mesh):
    data = P(None, ("fsdp", "rep"), None, None)
    ids = P(None, ("fsdp", "rep"))
    two = P(None, "fsdp")
    three = P(None, "fsdp", None)
    layer = (three, two) * 5
    in_specs = (data, data, ids, ids, ids, two, two) + layer
    out_specs = (data, data, two, two) + layer
    return jax.shard_map(
        on_device, mesh=mesh, in_specs=in_specs, out_specs=out_specs, check_vma=False
    )
```
